32 devices in a mesh: tm: 8 (over z, x), tensor: 4 (over y, core).
Axes of the slice: x: 2, y: 2, z: 4, core: 2. Of those that a mesh axis runs over, the one named last changes fastest.
Arguments:
- frames: bfloat16 [8192, 3072], P('tm', 'tensor'), may hold values from -9 to 9
- w_query: bfloat16 [3072, 2048], P(None, 'tensor'), may hold values from -0.09111309 to 0.09111309
- w_key: bfloat16 [3072, 2048], P(None, 'tensor'), may hold values from -0.12719748 to 0.12719748
- w_value: bfloat16 [3072, 2048], P(None, 'tensor'), may hold values from -0.109375 to 0.109375
- w_out: bfloat16 [2048, 3072], P('tensor'), may hold values from -0.125 to 0.125
- head_gain: float32 [3072], P('tensor'), may hold values from 0.25 to 1.75
- reward_weight: float32 [3072, 255], P('tensor'), may hold values from -0.75 to 0.75
- term_weight: float32 [3072], P('tensor'), may hold values from -0.109375 to 0.109375
- out_grad: bfloat16 [8192, 3072], P('tm', 'tensor'), may hold values from -0.75 to 0.75
- reward_bins: int32 [16], P('tm'), may hold values from 0 to 254
- episode_flags: int32 [16], P('tm'), may hold values from 0 to 2
Outputs:
- mixed: bfloat16 [8192, 3072], P('tm', 'tensor')
- pair_losses: float32 [2, 16], P(None, 'tm')
- grad_query: float32 [3072, 2048], P('tm', 'tensor')
- grad_key: float32 [3072, 2048], P('tm', 'tensor')
- grad_value: float32 [3072, 2048], P('tm', 'tensor')
- grad_out: float32 [2048, 3072], P('tensor', 'tm')
- grad_reward: float32 [3072, 255], P('tensor')
- grad_term: float32 [3072], P('tensor')
- grad_gain: float32 [3072], P('tensor')
The draws below stay inside these ranges and needn't reach their ends.
Inputs may be any that keep to these rules, and one draw needn't show every extreme that they name: `episode_flags`: 0: the episode goes on over the pair, 1: it terminates at the pair, 2: the pair straddles a reset and is left out.
All inputs are finite; a program needn't handle non-finite values.
Results may differ from the reference program's by a relative error of at most 0.024.
Values may be sent and summed in bfloat16 or wider, within the bound.
A program may use at most 128 MiB of HBM per device.

```python
import jax
import jax.numpy as jnp
from jax import lax

D = 3072
HEADS = 16
HD = 128
BINS = 255
PATCHES = 512
FRAMES = 16
ROWS = 8192
N_TENSOR = 4


def shared_query(key):
    normal = jax.random.truncated_normal(jax.random.fold_in(key, 100), -5.0, 5.0, (D, HEADS * HD), jnp.float32)
    return normal * D ** (-0.5)


def draw_w_query(key, part):
    common = shared_query(key)
    return common.astype(jnp.bfloat16)


def draw_w_key(key, part):
    key = jax.random.fold_in(key, 2)
    own = jax.random.truncated_normal(key, -5.0, 5.0, (D, HEADS * HD), jnp.float32) * D ** (-0.5)
    mixed_draw = own
    return mixed_draw.astype(jnp.bfloat16)


def draw_frames(key, part):
    key = jax.random.fold_in(key, 3)
    first = jax.random.fold_in(key, 0)
    values = jax.random.truncated_normal(first, -6.0, 6.0, (ROWS, D), jnp.float32)
    return values.astype(jnp.bfloat16)


def touch_ends(entries, key, low, largest):
    longest = entries.shape.index(max(entries.shape))
    spots = []
    for shift in (0, 1):
        where = [jax.random.randint(jax.random.fold_in(key, axis), (), 0, length) for axis, length in enumerate(entries.shape)]
        where[longest] = (where[longest] + shift) % entries.shape[longest]
        spots.append(tuple(where))
    return entries.at[spots[0]].set(low).at[spots[1]].set(largest)


def levels(rng, extent, shards, smallest, top_value):
    def one(dim, shards_of):
        steps = jax.random.uniform(jax.random.fold_in(jax.random.fold_in(rng, 6), dim), (shards_of,), jnp.float32, smallest / len(shards), top_value / len(shards))
        return jnp.repeat(jnp.exp(steps), extent[dim] // shards_of).reshape((-1,) + (1,) * (len(extent) - dim - 1))

    level = one(*shards[0])
    for cut in shards[1:]:
        level = level * one(*cut)
    return level


def gaussian(own_key, dims, deviation, bound, pieces=(), held_as=jnp.bfloat16):
    drawn = jax.random.normal(own_key, dims, jnp.float32) * deviation
    if len(pieces) > 0:
        drawn = levels(own_key, dims, pieces, -0.22, 0.18) * drawn
    return jnp.clip(drawn, min=-bound, max=bound).astype(held_as)


def setup_inputs(seed: int = 0) -> dict:
    seeds = jax.random.split(jax.random.key(seed), 12)
    frames = draw_frames(jax.random.fold_in(seeds[11], 71), 0)
    w_query = draw_w_query(jax.random.fold_in(seeds[11], 71), 0)
    w_key = draw_w_key(jax.random.fold_in(seeds[11], 71), 0)
    w_value = gaussian(seeds[3], (D, HEADS * HD), D ** -0.5, 0.109375, ((1, 4),))
    w_out = gaussian(seeds[4], (HEADS * HD, D), (HEADS * HD) ** -0.5, 0.125, ((0, 4),))
    head_gain = jnp.clip(1.0 + 0.15 * jax.random.normal(seeds[5], (D,), jnp.float32), 0.25, 1.75)
    reward_weight = gaussian(seeds[6], (D, BINS), (3.0 * D ** -0.5), 0.75, ((0, 4),), jnp.float32)
    term_weight = gaussian(seeds[7], (D,), D ** -0.5, 0.109375, ((0, 4),), jnp.float32)
    out_grad = gaussian(seeds[8], (ROWS, D), 0.05, 0.75, ((0, 8), (1, 4)))
    reward_bins = touch_ends(jax.random.randint(seeds[9], (FRAMES,), 0, BINS), jax.random.fold_in(seeds[9], 1), 0, BINS - 1).astype(jnp.int32)
    episode_flags = touch_ends(jax.random.randint(seeds[10], (FRAMES,), 0, 3), jax.random.fold_in(seeds[10], 1), 0, 2).astype(jnp.int32)
    return {"frames": frames, "w_query": w_query, "w_key": w_key, "w_value": w_value, "w_out": w_out, "head_gain": head_gain, "reward_weight": reward_weight, "term_weight": term_weight, "out_grad": out_grad, "reward_bins": reward_bins, "episode_flags": episode_flags}


def reference(frames, w_query, w_key, w_value, w_out, head_gain, reward_weight, term_weight, out_grad, reward_bins, episode_flags):
    f32 = jnp.float32
    bf16 = jnp.bfloat16
    highest = lax.Precision.HIGHEST
    width = HEADS * HD
    scale_qk = HD ** (-0.5)
    queries = jnp.dot(frames, w_query, preferred_element_type=f32).astype(bf16)
    keys = jnp.dot(frames, w_key, preferred_element_type=f32).astype(bf16)
    values = jnp.dot(frames, w_value, preferred_element_type=f32).astype(bf16)
    keys_pad = jnp.concatenate([keys, jnp.zeros((PATCHES, width), bf16)], 0)
    values_pad = jnp.concatenate([values, jnp.zeros((PATCHES, width), bf16)], 0)
    frames_pad = jnp.concatenate([frames, jnp.zeros((PATCHES, D), bf16)], 0)
    key_index = jnp.arange(2 * PATCHES, dtype=jnp.int32)

    def pair_probs(step):
        start = (step * PATCHES).astype(jnp.int32)
        query_rows = lax.dynamic_slice_in_dim(queries, start, PATCHES, 0).reshape(PATCHES, HEADS, HD)
        key_rows = lax.dynamic_slice_in_dim(keys_pad, start, 2 * PATCHES, 0).reshape(2 * PATCHES, HEADS, HD)
        value_rows = lax.dynamic_slice_in_dim(values_pad, start, 2 * PATCHES, 0).reshape(2 * PATCHES, HEADS, HD)
        scores = jnp.einsum('qhd,khd->hqk', query_rows.astype(f32), key_rows.astype(f32)) * scale_qk
        cut = (step == FRAMES - 1) & (key_index >= PATCHES)
        scores = jnp.where(cut[None, None, :], -1e+30, scores)
        probs = jax.nn.softmax(scores, axis=-1)
        return (query_rows, key_rows, value_rows, probs, start)

    def forward_pair(step):
        query_rows, key_rows, value_rows, probs, start = pair_probs(step)
        weights = probs.astype(bf16)
        out = jnp.einsum('hqk,khd->qhd', weights.astype(f32), value_rows.astype(f32))
        return out.astype(bf16).reshape(PATCHES, width)
    attended = lax.map(forward_pair, jnp.arange(FRAMES, dtype=jnp.int32)).reshape(ROWS, width)
    group = width // N_TENSOR

    def add_group(total, index):
        start = (index * group).astype(jnp.int32)
        cols = lax.dynamic_slice_in_dim(attended, start, group, 1)
        rows_w = lax.dynamic_slice_in_dim(w_out, start, group, 0)
        part = jnp.dot(cols, rows_w, preferred_element_type=f32).astype(bf16)
        return (total + lax.optimization_barrier(part).astype(f32), None)
    summed, _ = lax.scan(add_group, jnp.zeros((ROWS, D), f32), jnp.arange(N_TENSOR, dtype=jnp.int32))
    mixed = (frames.astype(f32) + summed).astype(bf16)
    pooled = mixed.astype(f32).reshape(FRAMES, PATCHES, D).mean(axis=1)
    scale = lax.rsqrt(lax.optimization_barrier(jnp.mean(pooled * pooled, axis=-1, keepdims=True)) + 1e-05)
    gained = pooled * head_gain[None, :]
    reward_logits = scale * jnp.dot(gained, reward_weight, precision=highest)
    term_logit = scale[:, 0] * jnp.dot(gained, term_weight, precision=highest)
    frame_ids = jnp.arange(FRAMES, dtype=jnp.int32)
    live = ((episode_flags != 2) & (frame_ids < FRAMES - 1)).astype(f32)
    target = (episode_flags == 1).astype(f32)
    onehot = (reward_bins[:, None] == jnp.arange(BINS, dtype=jnp.int32)[None, :]).astype(f32)
    reward_loss = live * (jax.scipy.special.logsumexp(reward_logits, axis=-1) - lax.optimization_barrier(jnp.sum(onehot * reward_logits, axis=-1)))
    term_loss = live * (jax.nn.softplus(term_logit) - target * term_logit)
    pair_losses = jnp.stack([reward_loss, term_loss])
    logit_grad = live[:, None] * (jax.nn.softmax(reward_logits, axis=-1) - onehot)
    term_grad = live * (jax.nn.sigmoid(term_logit) - target)
    scale_grad = (lax.optimization_barrier(jnp.sum(logit_grad * reward_logits, axis=-1)) + term_grad * term_logit) / scale[:, 0]
    gain_input_grad = scale * (jnp.dot(logit_grad, reward_weight.T, precision=highest) + term_grad[:, None] * term_weight[None, :])
    pooled_grad = head_gain[None, :] * gain_input_grad - scale_grad[:, None] * scale ** 3 * pooled / D
    grad_reward = jnp.dot(gained.T, scale * logit_grad, precision=highest)
    grad_term = jnp.dot(gained.T, scale[:, 0] * term_grad, precision=highest)
    grad_gain = lax.optimization_barrier(jnp.sum(pooled * gain_input_grad, axis=0))
    mixed_grad = (out_grad.astype(f32).reshape(FRAMES, PATCHES, D) + pooled_grad[:, None, :] / PATCHES).reshape(ROWS, D).astype(bf16)
    grad_out = jnp.dot(attended.T, mixed_grad, preferred_element_type=f32)
    attended_grad = jnp.dot(mixed_grad, w_out.T, preferred_element_type=f32).astype(bf16)

    def backward_pair(carry, step):
        grad_k, grad_v = carry
        query_rows, key_rows, value_rows, probs, start = pair_probs(step)
        weights = probs.astype(bf16)
        out_rows = lax.dynamic_slice_in_dim(attended_grad, start, PATCHES, 0).reshape(PATCHES, HEADS, HD)
        prob_grad = jnp.einsum('qhd,khd->hqk', out_rows.astype(f32), value_rows.astype(f32))
        value_pair = jnp.einsum('hqk,qhd->khd', weights.astype(f32), out_rows.astype(f32)).astype(bf16)
        delta = lax.optimization_barrier(jnp.sum(prob_grad * probs, axis=-1, keepdims=True))
        score_grad = (probs * (prob_grad - delta) * scale_qk).astype(bf16)
        query_grad = jnp.einsum('hqk,khd->qhd', score_grad.astype(f32), key_rows.astype(f32)).astype(bf16)
        key_pair = jnp.einsum('hqk,qhd->khd', score_grad.astype(f32), query_rows.astype(f32)).astype(bf16)
        key_feats = lax.dynamic_slice_in_dim(frames_pad, start, 2 * PATCHES, 0)
        grad_k = grad_k + jnp.dot(key_feats.T, key_pair.reshape(2 * PATCHES, width), preferred_element_type=f32)
        grad_v = grad_v + jnp.dot(key_feats.T, value_pair.reshape(2 * PATCHES, width), preferred_element_type=f32)
        return ((grad_k, grad_v), query_grad.reshape(PATCHES, width))
    start_grads = (jnp.zeros((D, width), f32), jnp.zeros((D, width), f32))
    (grad_key, grad_value), query_grads = lax.scan(backward_pair, start_grads, jnp.arange(FRAMES, dtype=jnp.int32))
    grad_query = jnp.dot(frames.T, query_grads.reshape(ROWS, width), preferred_element_type=f32)
    return (mixed, pair_losses, grad_query, grad_key, grad_value, grad_out, grad_reward, grad_term, grad_gain)
```

```python
import jax
import jax.numpy as jnp
from jax import lax
from jax.experimental import pallas as pl
from jax.experimental.pallas import tpu as pltpu
from jax.sharding import PartitionSpec as P

HD = 128
PATCHES = 512
NT = (((1,), (1,)), ((), ()))
TN = (((0,), (0,)), ((), ()))


def mm(left, right, dims=(((1,), (0,)), ((), ()))):
    return lax.dot_general(left, right, dims, preferred_element_type=jnp.float32)


def from_behind(x, axis, by):
    size = lax.axis_size(axis)
    pairs = [(i, i + by) for i in range(size) if 0 <= i + by < size]
    return lax.ppermute(x, axis, pairs)


def swap(x, axis, bit):
    return lax.ppermute(x, axis, [(i, i ^ bit) for i in range(lax.axis_size(axis))])


def ordered(flag, first, second):
    return jnp.where(
        flag == 0,
        jnp.concatenate([first, second], 1),
        jnp.concatenate([second, first], 1),
    )


def gather_tensor(x, me):
    if lax.axis_size("tensor") != 4:
        return lax.all_gather(x, "tensor", axis=1, tiled=True)
    far = swap(x, "tensor", 2)
    near = swap(x, "tensor", 1)
    far_near = swap(far, "tensor", 1)
    core, chip = me % 2, me // 2
    return ordered(chip, ordered(core, x, near), ordered(core, far, far_near))


def scatter_tensor(x, me):
    if lax.axis_size("tensor") != 4:
        return lax.psum_scatter(x, "tensor", scatter_dimension=1, tiled=True).astype(jnp.float32)
    f32 = jnp.float32
    core, chip = me % 2, me // 2
    quarter = x.shape[1] // 4
    part = [x[:, j * quarter : (j + 1) * quarter] for j in range(4)]
    even = jnp.concatenate([part[0], part[2]], 0)
    odd = jnp.concatenate([part[1], part[3]], 0)
    got = swap(jnp.where(core == 0, odd, even), "tensor", 1)
    own = jnp.where(core == 0, even, odd).astype(f32) + got.astype(f32)
    rows = x.shape[0]
    low, high = own[:rows], own[rows:]
    got = swap(jnp.where(chip == 0, high, low).astype(x.dtype), "tensor", 2)
    return jnp.where(chip == 0, low, high) + got.astype(f32)


def scatter_tm(x, position):
    f32 = jnp.float32
    size = lax.axis_size("tm")
    outer = size // 2
    rows, width = x.shape
    x = x.reshape(outer, 2, rows // size, width)
    side, place = position % 2, position // 2
    keep = lax.dynamic_index_in_dim(x, side, 1, keepdims=False)
    give = lax.dynamic_index_in_dim(x, 1 - side, 1, keepdims=False)
    acc = (keep.astype(f32) + swap(give, "tm", 1).astype(f32)).astype(x.dtype)

    def chunk(index):
        return lax.dynamic_index_in_dim(acc, jnp.clip(index, 0, outer - 1), 0, keepdims=False)

    right = left = None
    for step in range(outer - 1):
        reach = outer - 1 - step
        send_right, send_left = chunk(place + reach), chunk(place - reach)
        if right is not None:
            send_right = (send_right.astype(f32) + right.astype(f32)).astype(x.dtype)
            send_left = (send_left.astype(f32) + left.astype(f32)).astype(x.dtype)
        to_right = [(o, o + 1) for o in range(step + 1)]
        to_left = [(outer - 1 - a, outer - 1 - b) for a, b in to_right]
        both = range(2)
        right = lax.ppermute(
            send_right, "tm", [(2 * a + s, 2 * b + s) for a, b in to_right for s in both]
        )
        left = lax.ppermute(
            send_left, "tm", [(2 * a + s, 2 * b + s) for a, b in to_left for s in both]
        )
    total = chunk(place).astype(f32)
    if right is not None:
        total = total + right.astype(f32) + left.astype(f32)
    return total


def pair_probs(cut_ref, query, key_a, key_b):
    scale = HD ** (-0.5)
    score_a = mm(query, key_a, NT) * scale
    score_b = mm(query, key_b, NT) * scale
    score_b = jnp.where(cut_ref[0] != 0, -1e30, score_b)
    top = jnp.maximum(
        jnp.max(score_a, axis=-1, keepdims=True), jnp.max(score_b, axis=-1, keepdims=True)
    )
    exp_a, exp_b = jnp.exp(score_a - top), jnp.exp(score_b - top)
    total = jnp.sum(exp_a, axis=-1, keepdims=True) + jnp.sum(exp_b, axis=-1, keepdims=True)
    inverse = 1.0 / total
    return exp_a * inverse, exp_b * inverse


def forward_kernel(cut_ref, q_ref, ka_ref, kb_ref, va_ref, vb_ref, out_ref):
    prob_a, prob_b = pair_probs(cut_ref, q_ref[...], ka_ref[...], kb_ref[...])
    out = mm(prob_a.astype(jnp.bfloat16), va_ref[...]) + mm(
        prob_b.astype(jnp.bfloat16), vb_ref[...]
    )
    out_ref[...] = out.astype(jnp.bfloat16)


def backward_kernel(
    cut_ref, q_ref, ka_ref, kb_ref, va_ref, vb_ref, do_ref,
    dq_ref, dka_ref, dkb_ref, dva_ref, dvb_ref,
):
    bf16 = jnp.bfloat16
    query, out_grad = q_ref[...], do_ref[...]
    prob_a, prob_b = pair_probs(cut_ref, query, ka_ref[...], kb_ref[...])
    grad_a, grad_b = mm(out_grad, va_ref[...], NT), mm(out_grad, vb_ref[...], NT)
    dva_ref[...] = mm(prob_a.astype(bf16), out_grad, TN).astype(bf16)
    dvb_ref[...] = mm(prob_b.astype(bf16), out_grad, TN).astype(bf16)
    delta = jnp.sum(grad_a * prob_a, axis=-1, keepdims=True) + jnp.sum(
        grad_b * prob_b, axis=-1, keepdims=True
    )
    scale = HD ** (-0.5)
    score_a = (prob_a * (grad_a - delta) * scale).astype(bf16)
    score_b = (prob_b * (grad_b - delta) * scale).astype(bf16)
    dq_ref[...] = (mm(score_a, ka_ref[...]) + mm(score_b, kb_ref[...])).astype(bf16)
    dka_ref[...] = mm(score_a, query, TN).astype(bf16)
    dkb_ref[...] = mm(score_b, query, TN).astype(bf16)


def attention(kernel, outputs, cut, *arrays):
    rows, width = arrays[0].shape
    block = pl.BlockSpec((rows, HD), lambda head: (0, head))
    shape = jax.ShapeDtypeStruct((rows, width), jnp.bfloat16)
    work = 4 if outputs == 1 else 10
    return pl.pallas_call(
        kernel,
        grid=(width // HD,),
        in_specs=[pl.BlockSpec(memory_space=pltpu.SMEM)] + [block] * len(arrays),
        out_specs=[block] * outputs,
        out_shape=[shape] * outputs,
        compiler_params=pltpu.CompilerParams(vmem_limit_bytes=40 * 1024 * 1024),
        cost_estimate=pl.CostEstimate(
            flops=2 * work * rows * rows * width,
            bytes_accessed=2 * rows * width * (len(arrays) + outputs),
            transcendentals=2 * rows * rows * (width // HD),
        ),
    )(cut, *arrays)


def local(
    frames,
    w_query,
    w_key,
    w_value,
    w_out,
    head_gain,
    reward_weight,
    term_weight,
    out_grad,
    reward_bins,
    episode_flags,
):
    f32 = jnp.float32
    bf16 = jnp.bfloat16
    highest = lax.Precision.HIGHEST
    rows, local_width = frames.shape
    span = PATCHES
    pairs = rows // span
    width = w_query.shape[1]
    full_width = w_out.shape[1]
    tm_count = lax.axis_size("tm")
    position = lax.axis_index("tm")
    is_last = position == tm_count - 1
    frame_total = tm_count * pairs
    me = lax.axis_index("tensor")
    none = jnp.zeros((1,), jnp.int32)
    cuts = [none] * (pairs - 1) + [is_last.astype(jnp.int32).reshape(1)]
    feats = [
        gather_tensor(frames[index * span : (index + 1) * span], me) for index in range(pairs)
    ]
    keys = [mm(feat, w_key).astype(bf16) for feat in feats[:1]]
    values = [mm(feat, w_value).astype(bf16) for feat in feats[:1]]
    ahead = from_behind(jnp.concatenate([keys[0], values[0]], 1), "tm", -1)
    keys += [mm(feat, w_key).astype(bf16) for feat in feats[1:]] + [ahead[:, :width]]
    values += [mm(feat, w_value).astype(bf16) for feat in feats[1:]] + [ahead[:, width:]]
    queries = [mm(feat, w_query).astype(bf16) for feat in feats]
    late_grad, _ = lax.optimization_barrier((out_grad, feats[-1]))
    all_out_grad = lax.all_gather(late_grad, "tensor", axis=1, tiled=True)
    attended, mixed = [], []
    for index in range(pairs):
        (heads_out,) = attention(
            forward_kernel,
            1,
            cuts[index],
            queries[index],
            keys[index],
            keys[index + 1],
            values[index],
            values[index + 1],
        )
        attended.append(heads_out)
        summed = scatter_tensor(mm(heads_out, w_out).astype(bf16), me)
        own = frames[index * span : (index + 1) * span].astype(f32)
        mixed.append((own + summed).astype(bf16))
    mixed = jnp.concatenate(mixed, 0)
    attended = jnp.concatenate(attended, 0)
    gathered = jnp.concatenate(feats, 0)
    pooled = mixed.astype(f32).reshape(pairs, span, local_width).mean(axis=1)
    gained = pooled * head_gain[None, :]
    square_part = jnp.sum(pooled * pooled, axis=-1)
    raw_reward = jnp.dot(gained, reward_weight, precision=highest)
    raw_term = jnp.dot(gained, term_weight, precision=highest)
    sums = lax.psum(
        jnp.concatenate([raw_reward, raw_term[:, None], square_part[:, None]], 1), "tensor"
    )
    bins_count = reward_weight.shape[1]
    scale = lax.rsqrt(sums[:, bins_count + 1] / full_width + 1e-05)
    reward_logits = scale[:, None] * sums[:, :bins_count]
    term_logit = scale * sums[:, bins_count]
    frame_ids = position * pairs + jnp.arange(pairs, dtype=jnp.int32)
    live = ((episode_flags != 2) & (frame_ids < frame_total - 1)).astype(f32)
    target = (episode_flags == 1).astype(f32)
    onehot = (reward_bins[:, None] == jnp.arange(bins_count, dtype=jnp.int32)[None, :]).astype(f32)
    reward_loss = live * (
        jax.scipy.special.logsumexp(reward_logits, axis=-1)
        - jnp.sum(onehot * reward_logits, axis=-1)
    )
    term_loss = live * (jax.nn.softplus(term_logit) - target * term_logit)
    pair_losses = jnp.stack([reward_loss, term_loss])
    logit_grad = live[:, None] * (jax.nn.softmax(reward_logits, axis=-1) - onehot)
    term_grad = live * (jax.nn.sigmoid(term_logit) - target)
    scale_grad = (jnp.sum(logit_grad * reward_logits, axis=-1) + term_grad * term_logit) / scale
    gain_input_grad = scale[:, None] * (
        jnp.dot(logit_grad, reward_weight.T, precision=highest)
        + term_grad[:, None] * term_weight[None, :]
    )
    pooled_grad = (
        head_gain[None, :] * gain_input_grad
        - (scale_grad * scale**3)[:, None] * pooled / full_width
    )
    reward_part = jnp.dot(gained.T, scale[:, None] * logit_grad, precision=highest)
    term_part = jnp.dot(gained.T, scale * term_grad, precision=highest)
    gain_part = jnp.sum(pooled * gain_input_grad, axis=0)
    all_pooled_grad = lax.all_gather(pooled_grad, "tensor", axis=1, tiled=True)
    piece = (
        (
            all_out_grad.astype(f32).reshape(pairs, span, full_width)
            + all_pooled_grad[:, None, :] / span
        )
        .reshape(rows, full_width)
        .astype(bf16)
    )
    attended_grad = mm(piece, w_out, NT).astype(bf16)
    grads = [None] * pairs
    for index in reversed(range(pairs)):
        grads[index] = attention(
            backward_kernel,
            5,
            cuts[index],
            queries[index],
            keys[index],
            keys[index + 1],
            values[index],
            values[index + 1],
            attended_grad[index * span : (index + 1) * span],
        )
        if index == pairs - 1:
            passed = from_behind(jnp.concatenate([grads[index][2], grads[index][4]], 1), "tm", 1)
    grad_out = scatter_tm(mm(piece, attended, TN).astype(bf16), position).T
    small = lax.psum(
        jnp.concatenate([reward_part, term_part[:, None], gain_part[:, None]], 1).astype(bf16),
        "tm",
    ).astype(f32)
    grad_reward, grad_term, grad_gain = (
        small[:, :bins_count],
        small[:, bins_count],
        small[:, bins_count + 1],
    )
    query_grad = jnp.concatenate([grad[0] for grad in grads], 0)
    grad_query = scatter_tm(mm(gathered, query_grad, TN).astype(bf16), position)

    def joined(first, second, behind):
        late = [behind] + [grad[second] for grad in grads[:-1]]
        return jnp.concatenate(
            [
                (grad[first].astype(f32) + other.astype(f32)).astype(bf16)
                for grad, other in zip(grads, late)
            ],
            0,
        )

    value_grad = joined(3, 4, passed[:, width:])
    grad_value = scatter_tm(mm(gathered, value_grad, TN).astype(bf16), position)
    key_grad = joined(1, 2, passed[:, :width])
    grad_key = scatter_tm(mm(gathered, key_grad, TN).astype(bf16), position)
    return (
        mixed,
        pair_losses,
        grad_query,
        grad_key,
        grad_value,
        grad_out,
        grad_reward,
        grad_term,
        grad_gain,
    )


def solution(mesh):
    return jax.shard_map(
        local,
        mesh=mesh,
        in_specs=(
            P("tm", "tensor"),
            P(None, "tensor"),
            P(None, "tensor"),
            P(None, "tensor"),
            P("tensor", None),
            P("tensor"),
            P("tensor", None),
            P("tensor"),
            P("tm", "tensor"),
            P("tm"),
            P("tm"),
        ),
        out_specs=(
            P("tm", "tensor"),
            P(None, "tm"),
            P("tm", "tensor"),
            P("tm", "tensor"),
            P("tm", "tensor"),
            P("tensor", "tm"),
            P("tensor", None),
            P("tensor"),
            P("tensor"),
        ),
        check_vma=False,
    )
```

```python
import jax
import jax.numpy as jnp
from jax import lax
from jax.experimental import pallas as pl
from jax.experimental.pallas import tpu as pltpu
from jax.sharding import PartitionSpec as P

HD = 128
PATCHES = 512
NT = (((1,), (1,)), ((), ()))
TN = (((0,), (0,)), ((), ()))


def mm(left, right, dims=(((1,), (0,)), ((), ()))):
    return lax.dot_general(left, right, dims, preferred_element_type=jnp.float32)


def from_behind(x, axis, by):
    size = lax.axis_size(axis)
    pairs = [(i, i + by) for i in range(size) if 0 <= i + by < size]
    return lax.ppermute(x, axis, pairs)


def swap(x, axis, bit):
    return lax.ppermute(x, axis, [(i, i ^ bit) for i in range(lax.axis_size(axis))])


def tie(value, *others):
    return lax.optimization_barrier((value, *others))[0]


def twisted():
    return lax.axis_size("tensor") == 4 and lax.axis_size("tm") == 8


def twist_rows(weight, me):
    if not twisted():
        return weight
    quarter = weight.shape[0] // 4
    return jnp.concatenate(
        [
            lax.dynamic_slice_in_dim(weight, (me ^ j) * quarter, quarter, 0) for j in range(4)
        ],
        0,
    )


def ordered(flag, first, second):
    return jnp.where(
        flag == 0,
        jnp.concatenate([first, second], 1),
        jnp.concatenate([second, first], 1),
    )


def gather_tensor(x, me):
    if lax.axis_size("tensor") != 4:
        return lambda *_: lax.all_gather(x, "tensor", axis=1, tiled=True), x
    far = swap(x, "tensor", 2)
    near = swap(x, "tensor", 1)

    def finish(*after):
        arrived = tie(far, *after) if after else far
        far_near = swap(arrived, "tensor", 1)
        if twisted():
            return jnp.concatenate([x, near, arrived, far_near], 1)
        core, chip = me % 2, me // 2
        return ordered(chip, ordered(core, x, near), ordered(core, arrived, far_near))

    return finish, far


def scatter_cores(x, me):
    f32 = jnp.float32
    core, chip = me % 2, me // 2
    quarter = x.shape[1] // 4
    part = [x[:, j * quarter : (j + 1) * quarter] for j in range(4)]
    even = jnp.concatenate([part[0], part[2]], 0)
    odd = jnp.concatenate([part[1], part[3]], 0)
    got = swap(jnp.where(core == 0, odd, even), "tensor", 1)
    own = jnp.where(core == 0, even, odd).astype(f32) + got.astype(f32)
    rows = x.shape[0]
    low, high = own[:rows], own[rows:]
    return jnp.where(chip == 0, low, high), jnp.where(chip == 0, high, low).astype(x.dtype)


def scatter_tensor(x, me):
    if lax.axis_size("tensor") != 4:
        return lax.psum_scatter(x, "tensor", scatter_dimension=1, tiled=True).astype(jnp.float32), x
    keep, give = scatter_cores(x, me)
    return keep + swap(give, "tensor", 2).astype(jnp.float32), give


def scatter_tm(x, position, twist=0):
    f32 = jnp.float32
    size = lax.axis_size("tm")
    outer = size // 2
    rows, width = x.shape
    x = x.reshape(outer, 2, rows // size, width)
    side, place = position % 2, position // 2
    keep = lax.dynamic_index_in_dim(x, side, 1, keepdims=False)
    give = lax.dynamic_index_in_dim(x, 1 - side, 1, keepdims=False)
    acc = (keep.astype(f32) + swap(give, "tm", 1).astype(f32)).astype(x.dtype)

    def chunk(index):
        return lax.dynamic_index_in_dim(acc, jnp.clip(index, 0, outer - 1) ^ twist, 0, keepdims=False)

    right = left = None
    for step in range(outer - 1):
        reach = outer - 1 - step
        send_right, send_left = chunk(place + reach), chunk(place - reach)
        if right is not None:
            send_right = (send_right.astype(f32) + right.astype(f32)).astype(x.dtype)
            send_left = (send_left.astype(f32) + left.astype(f32)).astype(x.dtype)
        to_right = [(o, o + 1) for o in range(step + 1)]
        to_left = [(outer - 1 - a, outer - 1 - b) for a, b in to_right]
        both = range(2)
        right = lax.ppermute(
            send_right, "tm", [(2 * a + s, 2 * b + s) for a, b in to_right for s in both]
        )
        left = lax.ppermute(
            send_left, "tm", [(2 * a + s, 2 * b + s) for a, b in to_left for s in both]
        )
    total = chunk(place).astype(f32)
    if right is not None:
        total = total + right.astype(f32) + left.astype(f32)
    return total


def pair_probs(cut_ref, query, key_a, key_b):
    scale = HD ** (-0.5)
    score_a = mm(query, key_a, NT) * scale
    score_b = mm(query, key_b, NT) * scale
    score_b = jnp.where(cut_ref[0] != 0, -1e30, score_b)
    top = jnp.maximum(
        jnp.max(score_a, axis=-1, keepdims=True), jnp.max(score_b, axis=-1, keepdims=True)
    )
    exp_a, exp_b = jnp.exp(score_a - top), jnp.exp(score_b - top)
    total = jnp.sum(exp_a, axis=-1, keepdims=True) + jnp.sum(exp_b, axis=-1, keepdims=True)
    inverse = 1.0 / total
    return exp_a * inverse, exp_b * inverse


def forward_kernel(cut_ref, q_ref, ka_ref, kb_ref, va_ref, vb_ref, out_ref):
    prob_a, prob_b = pair_probs(cut_ref, q_ref[...], ka_ref[...], kb_ref[...])
    out = mm(prob_a.astype(jnp.bfloat16), va_ref[...]) + mm(
        prob_b.astype(jnp.bfloat16), vb_ref[...]
    )
    out_ref[...] = out.astype(jnp.bfloat16)


def backward_kernel(
    cut_ref, q_ref, ka_ref, kb_ref, va_ref, vb_ref, do_ref,
    dq_ref, dka_ref, dkb_ref, dva_ref, dvb_ref,
):
    bf16 = jnp.bfloat16
    query, out_grad = q_ref[...], do_ref[...]
    prob_a, prob_b = pair_probs(cut_ref, query, ka_ref[...], kb_ref[...])
    grad_a, grad_b = mm(out_grad, va_ref[...], NT), mm(out_grad, vb_ref[...], NT)
    dva_ref[...] = mm(prob_a.astype(bf16), out_grad, TN).astype(bf16)
    dvb_ref[...] = mm(prob_b.astype(bf16), out_grad, TN).astype(bf16)
    delta = jnp.sum(grad_a * prob_a, axis=-1, keepdims=True) + jnp.sum(
        grad_b * prob_b, axis=-1, keepdims=True
    )
    scale = HD ** (-0.5)
    score_a = (prob_a * (grad_a - delta) * scale).astype(bf16)
    score_b = (prob_b * (grad_b - delta) * scale).astype(bf16)
    dq_ref[...] = (mm(score_a, ka_ref[...]) + mm(score_b, kb_ref[...])).astype(bf16)
    dka_ref[...] = mm(score_a, query, TN).astype(bf16)
    dkb_ref[...] = mm(score_b, query, TN).astype(bf16)


def attention(kernel, outputs, cut, *arrays):
    rows, width = arrays[0].shape
    block = pl.BlockSpec((rows, HD), lambda head: (0, head))
    shape = jax.ShapeDtypeStruct((rows, width), jnp.bfloat16)
    work = 4 if outputs == 1 else 10
    return pl.pallas_call(
        kernel,
        grid=(width // HD,),
        in_specs=[pl.BlockSpec(memory_space=pltpu.SMEM)] + [block] * len(arrays),
        out_specs=[block] * outputs,
        out_shape=[shape] * outputs,
        compiler_params=pltpu.CompilerParams(vmem_limit_bytes=40 * 1024 * 1024),
        cost_estimate=pl.CostEstimate(
            flops=8 * work * rows * rows * width,
            bytes_accessed=2 * rows * width * (len(arrays) + outputs),
            transcendentals=2 * rows * rows * (width // HD),
        ),
    )(cut, *arrays)


def local(
    frames,
    w_query,
    w_key,
    w_value,
    w_out,
    head_gain,
    reward_weight,
    term_weight,
    out_grad,
    reward_bins,
    episode_flags,
):
    f32 = jnp.float32
    bf16 = jnp.bfloat16
    highest = lax.Precision.HIGHEST
    rows, local_width = frames.shape
    span = PATCHES
    pairs = rows // span
    width = w_query.shape[1]
    full_width = w_out.shape[1]
    tm_count = lax.axis_size("tm")
    position = lax.axis_index("tm")
    is_last = position == tm_count - 1
    frame_total = tm_count * pairs
    me = lax.axis_index("tensor")
    none = jnp.zeros((1,), jnp.int32)
    cuts = [none] * (pairs - 1) + [is_last.astype(jnp.int32).reshape(1)]
    twist = me if twisted() else 0
    row_query, row_key, row_value = (twist_rows(w, me) for w in (w_query, w_key, w_value))
    started = [
        gather_tensor(frames[index * span : (index + 1) * span], me) for index in range(pairs)
    ]
    feats, queries, keys, values = [], [], [], []
    ready = ()
    for index in range(pairs):
        feat = started[index][0](*ready)
        keys.append(mm(feat, row_key).astype(bf16))
        values.append(mm(feat, row_value).astype(bf16))
        queries.append(mm(feat, row_query).astype(bf16))
        if index == 0:
            first = jnp.concatenate([keys[0], values[0]], 1)
            ahead = from_behind(first, "tm", -1)
        ready = (first, queries[index])
        feats.append(feat)
    keys.append(ahead[:, :width])
    values.append(ahead[:, width:])
    late_grad = tie(out_grad, started[-1][1])
    all_out_grad = lax.all_gather(late_grad, "tensor", axis=1, tiled=True)
    attended, mixed = [], []
    given = None
    for index in range(pairs):
        if given is not None:
            queries[index] = tie(queries[index], given)
        (heads_out,) = attention(
            forward_kernel,
            1,
            cuts[index],
            queries[index],
            keys[index],
            keys[index + 1],
            values[index],
            values[index + 1],
        )
        attended.append(heads_out)
        summed, given = scatter_tensor(mm(heads_out, w_out).astype(bf16), me)
        own = frames[index * span : (index + 1) * span].astype(f32)
        mixed.append((own + summed).astype(bf16))
    mixed = jnp.concatenate(mixed, 0)
    attended = jnp.concatenate(attended, 0)
    gathered = jnp.concatenate(feats, 0)
    pooled = mixed.astype(f32).reshape(pairs, span, local_width).mean(axis=1)
    gained = pooled * head_gain[None, :]
    square_part = jnp.sum(pooled * pooled, axis=-1)
    raw_reward = jnp.dot(gained, reward_weight, precision=highest)
    raw_term = jnp.dot(gained, term_weight, precision=highest)
    sums = lax.psum(
        jnp.concatenate([raw_reward, raw_term[:, None], square_part[:, None]], 1), "tensor"
    )
    bins_count = reward_weight.shape[1]
    scale = lax.rsqrt(sums[:, bins_count + 1] / full_width + 1e-05)
    reward_logits = scale[:, None] * sums[:, :bins_count]
    term_logit = scale * sums[:, bins_count]
    frame_ids = position * pairs + jnp.arange(pairs, dtype=jnp.int32)
    live = ((episode_flags != 2) & (frame_ids < frame_total - 1)).astype(f32)
    target = (episode_flags == 1).astype(f32)
    onehot = (reward_bins[:, None] == jnp.arange(bins_count, dtype=jnp.int32)[None, :]).astype(f32)
    reward_loss = live * (
        jax.scipy.special.logsumexp(reward_logits, axis=-1)
        - jnp.sum(onehot * reward_logits, axis=-1)
    )
    term_loss = live * (jax.nn.softplus(term_logit) - target * term_logit)
    pair_losses = jnp.stack([reward_loss, term_loss])
    logit_grad = live[:, None] * (jax.nn.softmax(reward_logits, axis=-1) - onehot)
    term_grad = live * (jax.nn.sigmoid(term_logit) - target)
    scale_grad = (jnp.sum(logit_grad * reward_logits, axis=-1) + term_grad * term_logit) / scale
    gain_input_grad = scale[:, None] * (
        jnp.dot(logit_grad, reward_weight.T, precision=highest)
        + term_grad[:, None] * term_weight[None, :]
    )
    pooled_grad = (
        head_gain[None, :] * gain_input_grad
        - (scale_grad * scale**3)[:, None] * pooled / full_width
    )
    reward_part = jnp.dot(gained.T, scale[:, None] * logit_grad, precision=highest)
    term_part = jnp.dot(gained.T, scale * term_grad, precision=highest)
    gain_part = jnp.sum(pooled * gain_input_grad, axis=0)
    all_pooled_grad = lax.all_gather(pooled_grad, "tensor", axis=1, tiled=True)
    piece = (
        (
            all_out_grad.astype(f32).reshape(pairs, span, full_width)
            + all_pooled_grad[:, None, :] / span
        )
        .reshape(rows, full_width)
        .astype(bf16)
    )
    out_product = mm(piece, attended, TN).astype(bf16)
    attended_grad = mm(tie(piece, out_product), w_out, NT).astype(bf16)
    grads = [None] * pairs
    sent = None
    for index in reversed(range(pairs)):
        asked = queries[index] if sent is None else tie(queries[index], sent)
        grads[index] = attention(
            backward_kernel,
            5,
            cuts[index],
            asked,
            keys[index],
            keys[index + 1],
            values[index],
            values[index + 1],
            attended_grad[index * span : (index + 1) * span],
        )
        if index == pairs - 1:
            sent = jnp.concatenate([grads[index][2], grads[index][4]], 1)
            passed = from_behind(sent, "tm", 1)
    grad_out = scatter_tm(out_product, position).T
    small = lax.psum(
        jnp.concatenate([reward_part, term_part[:, None], gain_part[:, None]], 1).astype(bf16),
        "tm",
    ).astype(f32)
    grad_reward, grad_term, grad_gain = (
        small[:, :bins_count],
        small[:, bins_count],
        small[:, bins_count + 1],
    )
    query_grad = jnp.concatenate([grad[0] for grad in grads], 0)
    grad_query = scatter_tm(mm(gathered, query_grad, TN).astype(bf16), position, twist)

    def joined(first, second, behind):
        late = [behind] + [grad[second] for grad in grads[:-1]]
        return jnp.concatenate(
            [
                (grad[first].astype(f32) + other.astype(f32)).astype(bf16)
                for grad, other in zip(grads, late)
            ],
            0,
        )

    value_grad = joined(3, 4, passed[:, width:])
    grad_value = scatter_tm(mm(gathered, value_grad, TN).astype(bf16), position, twist)
    key_grad = joined(1, 2, passed[:, :width])
    grad_key = scatter_tm(mm(gathered, key_grad, TN).astype(bf16), position, twist)
    return (
        mixed,
        pair_losses,
        grad_query,
        grad_key,
        grad_value,
        grad_out,
        grad_reward,
        grad_term,
        grad_gain,
    )


def solution(mesh):
    return jax.shard_map(
        local,
        mesh=mesh,
        in_specs=(
            P("tm", "tensor"),
            P(None, "tensor"),
            P(None, "tensor"),
            P(None, "tensor"),
            P("tensor", None),
            P("tensor"),
            P("tensor", None),
            P("tensor"),
            P("tm", "tensor"),
            P("tm"),
            P("tm"),
        ),
        out_specs=(
            P("tm", "tensor"),
            P(None, "tm"),
            P("tm", "tensor"),
            P("tm", "tensor"),
            P("tm", "tensor"),
            P("tensor", "tm"),
            P("tensor", None),
            P("tensor"),
            P("tensor"),
        ),
        check_vma=False,
    )
```

```python
import jax
import jax.numpy as jnp
from jax import lax
from jax.experimental import pallas as pl
from jax.experimental.pallas import tpu as pltpu
from jax.sharding import PartitionSpec as P

HD = 128
PATCHES = 512
NT = (((1,), (1,)), ((), ()))
TN = (((0,), (0,)), ((), ()))


def mm(left, right, dims=(((1,), (0,)), ((), ()))):
    return lax.dot_general(left, right, dims, preferred_element_type=jnp.float32)


def from_behind(x, axis, by):
    size = lax.axis_size(axis)
    pairs = [(i, i + by) for i in range(size) if 0 <= i + by < size]
    return lax.ppermute(x, axis, pairs)


def swap(x, axis, bit):
    return lax.ppermute(x, axis, [(i, i ^ bit) for i in range(lax.axis_size(axis))])


def tie(value, *others):
    return lax.optimization_barrier((value, *others))[0]


def twisted():
    return lax.axis_size("tensor") == 4 and lax.axis_size("tm") == 8


def twist_rows(weight, me):
    if not twisted():
        return weight
    quarter = weight.shape[0] // 4
    return jnp.concatenate(
        [
            lax.dynamic_slice_in_dim(weight, (me ^ j) * quarter, quarter, 0) for j in range(4)
        ],
        0,
    )


def ordered(flag, first, second):
    return jnp.where(
        flag == 0,
        jnp.concatenate([first, second], 1),
        jnp.concatenate([second, first], 1),
    )


def gather_tensor(x, me):
    if lax.axis_size("tensor") != 4:
        return lambda *_: lax.all_gather(x, "tensor", axis=1, tiled=True), x
    far = swap(x, "tensor", 2)
    near = swap(x, "tensor", 1)

    def finish(*after):
        arrived = tie(far, *after) if after else far
        far_near = swap(arrived, "tensor", 1)
        if twisted():
            return jnp.concatenate([x, near, arrived, far_near], 1)
        core, chip = me % 2, me // 2
        return ordered(chip, ordered(core, x, near), ordered(core, arrived, far_near))

    return finish, far


def scatter_cores(x, me):
    f32 = jnp.float32
    core, chip = me % 2, me // 2
    quarter = x.shape[1] // 4
    part = [x[:, j * quarter : (j + 1) * quarter] for j in range(4)]
    even = jnp.concatenate([part[0], part[2]], 0)
    odd = jnp.concatenate([part[1], part[3]], 0)
    got = swap(jnp.where(core == 0, odd, even), "tensor", 1)
    own = jnp.where(core == 0, even, odd).astype(f32) + got.astype(f32)
    rows = x.shape[0]
    low, high = own[:rows], own[rows:]
    return jnp.where(chip == 0, low, high), jnp.where(chip == 0, high, low).astype(x.dtype)


def scatter_tensor(x, me):
    if lax.axis_size("tensor") != 4:
        return lax.psum_scatter(x, "tensor", scatter_dimension=1, tiled=True).astype(jnp.float32), x
    keep, give = scatter_cores(x, me)
    return keep + swap(give, "tensor", 2).astype(jnp.float32), give


def halve_tm(x, position):
    size = lax.axis_size("tm")
    rows, width = x.shape
    x = x.reshape(size // 2, 2, rows // size, width)
    side = position % 2
    keep = lax.dynamic_index_in_dim(x, side, 1, keepdims=False)
    return keep, lax.dynamic_index_in_dim(x, 1 - side, 1, keepdims=False)


def scatter_tm(halves, position, twist=0, after=()):
    f32 = jnp.float32
    keep, give = halves
    size = lax.axis_size("tm")
    outer = size // 2
    place = position // 2
    got = swap(give, "tm", 1)
    if after:
        got = tie(got, *after)
    acc = (keep.astype(f32) + got.astype(f32)).astype(keep.dtype)

    def chunk(index):
        return lax.dynamic_index_in_dim(acc, jnp.clip(index, 0, outer - 1) ^ twist, 0, keepdims=False)

    right = left = None
    for step in range(outer - 1):
        reach = outer - 1 - step
        send_right, send_left = chunk(place + reach), chunk(place - reach)
        if right is not None:
            send_right = (send_right.astype(f32) + right.astype(f32)).astype(keep.dtype)
            send_left = (send_left.astype(f32) + left.astype(f32)).astype(keep.dtype)
        to_right = [(o, o + 1) for o in range(step + 1)]
        to_left = [(outer - 1 - a, outer - 1 - b) for a, b in to_right]
        both = range(2)
        right = lax.ppermute(
            send_right, "tm", [(2 * a + s, 2 * b + s) for a, b in to_right for s in both]
        )
        left = lax.ppermute(
            send_left, "tm", [(2 * a + s, 2 * b + s) for a, b in to_left for s in both]
        )
    total = chunk(place).astype(f32)
    if right is not None:
        total = total + right.astype(f32) + left.astype(f32)
    return total


def pair_probs(cut_ref, query, key_a, key_b):
    scale = HD ** (-0.5)
    score_a = mm(query, key_a, NT) * scale
    score_b = mm(query, key_b, NT) * scale
    score_b = jnp.where(cut_ref[0] != 0, -1e30, score_b)
    top = jnp.maximum(
        jnp.max(score_a, axis=-1, keepdims=True), jnp.max(score_b, axis=-1, keepdims=True)
    )
    exp_a, exp_b = jnp.exp(score_a - top), jnp.exp(score_b - top)
    total = jnp.sum(exp_a, axis=-1, keepdims=True) + jnp.sum(exp_b, axis=-1, keepdims=True)
    inverse = 1.0 / total
    return exp_a * inverse, exp_b * inverse


def forward_kernel(cut_ref, q_ref, ka_ref, kb_ref, va_ref, vb_ref, out_ref):
    prob_a, prob_b = pair_probs(cut_ref, q_ref[...], ka_ref[...], kb_ref[...])
    out = mm(prob_a.astype(jnp.bfloat16), va_ref[...]) + mm(
        prob_b.astype(jnp.bfloat16), vb_ref[...]
    )
    out_ref[...] = out.astype(jnp.bfloat16)


def backward_kernel(
    cut_ref, q_ref, ka_ref, kb_ref, va_ref, vb_ref, do_ref,
    dq_ref, dka_ref, dkb_ref, dva_ref, dvb_ref,
):
    bf16 = jnp.bfloat16
    query, out_grad = q_ref[...], do_ref[...]
    prob_a, prob_b = pair_probs(cut_ref, query, ka_ref[...], kb_ref[...])
    grad_a, grad_b = mm(out_grad, va_ref[...], NT), mm(out_grad, vb_ref[...], NT)
    dva_ref[...] = mm(prob_a.astype(bf16), out_grad, TN).astype(bf16)
    dvb_ref[...] = mm(prob_b.astype(bf16), out_grad, TN).astype(bf16)
    delta = jnp.sum(grad_a * prob_a, axis=-1, keepdims=True) + jnp.sum(
        grad_b * prob_b, axis=-1, keepdims=True
    )
    scale = HD ** (-0.5)
    score_a = (prob_a * (grad_a - delta) * scale).astype(bf16)
    score_b = (prob_b * (grad_b - delta) * scale).astype(bf16)
    dq_ref[...] = (mm(score_a, ka_ref[...]) + mm(score_b, kb_ref[...])).astype(bf16)
    dka_ref[...] = mm(score_a, query, TN).astype(bf16)
    dkb_ref[...] = mm(score_b, query, TN).astype(bf16)


def attention(kernel, outputs, cut, *arrays):
    rows, width = arrays[0].shape
    block = pl.BlockSpec((rows, HD), lambda head: (0, head))
    shape = jax.ShapeDtypeStruct((rows, width), jnp.bfloat16)
    work = 4 if outputs == 1 else 10
    return pl.pallas_call(
        kernel,
        grid=(width // HD,),
        in_specs=[pl.BlockSpec(memory_space=pltpu.SMEM)] + [block] * len(arrays),
        out_specs=[block] * outputs,
        out_shape=[shape] * outputs,
        compiler_params=pltpu.CompilerParams(vmem_limit_bytes=40 * 1024 * 1024),
        cost_estimate=pl.CostEstimate(
            flops=8 * work * rows * rows * width,
            bytes_accessed=2 * rows * width * (len(arrays) + outputs),
            transcendentals=2 * rows * rows * (width // HD),
        ),
    )(cut, *arrays)


def local(
    frames,
    w_query,
    w_key,
    w_value,
    w_out,
    head_gain,
    reward_weight,
    term_weight,
    out_grad,
    reward_bins,
    episode_flags,
):
    f32 = jnp.float32
    bf16 = jnp.bfloat16
    highest = lax.Precision.HIGHEST
    rows, local_width = frames.shape
    span = PATCHES
    pairs = rows // span
    width = w_query.shape[1]
    full_width = w_out.shape[1]
    tm_count = lax.axis_size("tm")
    position = lax.axis_index("tm")
    is_last = position == tm_count - 1
    frame_total = tm_count * pairs
    me = lax.axis_index("tensor")
    none = jnp.zeros((1,), jnp.int32)
    cuts = [none] * (pairs - 1) + [is_last.astype(jnp.int32).reshape(1)]
    twist = me if twisted() else 0
    row_query, row_key, row_value = (twist_rows(w, me) for w in (w_query, w_key, w_value))
    started = [
        gather_tensor(frames[index * span : (index + 1) * span], me) for index in range(pairs)
    ]
    feats, queries, keys, values = [], [], [], []
    ready = ()
    for index in range(pairs):
        feat = started[index][0](*ready)
        keys.append(mm(feat, row_key).astype(bf16))
        values.append(mm(feat, row_value).astype(bf16))
        queries.append(mm(feat, row_query).astype(bf16))
        if index == 0:
            first = jnp.concatenate([keys[0], values[0]], 1)
            ahead = from_behind(first, "tm", -1)
        ready = (first, queries[index])
        feats.append(feat)
    keys.append(ahead[:, :width])
    values.append(ahead[:, width:])
    late_grad = tie(out_grad, started[-1][1])
    all_out_grad = lax.all_gather(late_grad, "tensor", axis=1, tiled=True)
    attended, mixed = [], []
    given = None
    for index in range(pairs):
        if given is not None:
            queries[index] = tie(queries[index], given)
        (heads_out,) = attention(
            forward_kernel,
            1,
            cuts[index],
            queries[index],
            keys[index],
            keys[index + 1],
            values[index],
            values[index + 1],
        )
        attended.append(heads_out)
        summed, given = scatter_tensor(mm(heads_out, w_out).astype(bf16), me)
        own = frames[index * span : (index + 1) * span].astype(f32)
        mixed.append((own + summed).astype(bf16))
    mixed = jnp.concatenate(mixed, 0)
    attended = jnp.concatenate(attended, 0)
    gathered = jnp.concatenate(feats, 0)
    pooled = mixed.astype(f32).reshape(pairs, span, local_width).mean(axis=1)
    gained = pooled * head_gain[None, :]
    square_part = jnp.sum(pooled * pooled, axis=-1)
    raw_reward = jnp.dot(gained, reward_weight, precision=highest)
    raw_term = jnp.dot(gained, term_weight, precision=highest)
    sums = lax.psum(
        jnp.concatenate([raw_reward, raw_term[:, None], square_part[:, None]], 1), "tensor"
    )
    bins_count = reward_weight.shape[1]
    scale = lax.rsqrt(sums[:, bins_count + 1] / full_width + 1e-05)
    reward_logits = scale[:, None] * sums[:, :bins_count]
    term_logit = scale * sums[:, bins_count]
    frame_ids = position * pairs + jnp.arange(pairs, dtype=jnp.int32)
    live = ((episode_flags != 2) & (frame_ids < frame_total - 1)).astype(f32)
    target = (episode_flags == 1).astype(f32)
    onehot = (reward_bins[:, None] == jnp.arange(bins_count, dtype=jnp.int32)[None, :]).astype(f32)
    reward_loss = live * (
        jax.scipy.special.logsumexp(reward_logits, axis=-1)
        - jnp.sum(onehot * reward_logits, axis=-1)
    )
    term_loss = live * (jax.nn.softplus(term_logit) - target * term_logit)
    pair_losses = jnp.stack([reward_loss, term_loss])
    logit_grad = live[:, None] * (jax.nn.softmax(reward_logits, axis=-1) - onehot)
    term_grad = live * (jax.nn.sigmoid(term_logit) - target)
    scale_grad = (jnp.sum(logit_grad * reward_logits, axis=-1) + term_grad * term_logit) / scale
    gain_input_grad = scale[:, None] * (
        jnp.dot(logit_grad, reward_weight.T, precision=highest)
        + term_grad[:, None] * term_weight[None, :]
    )
    pooled_grad = (
        head_gain[None, :] * gain_input_grad
        - (scale_grad * scale**3)[:, None] * pooled / full_width
    )
    reward_part = jnp.dot(gained.T, scale[:, None] * logit_grad, precision=highest)
    term_part = jnp.dot(gained.T, scale * term_grad, precision=highest)
    gain_part = jnp.sum(pooled * gain_input_grad, axis=0)
    all_pooled_grad = lax.all_gather(pooled_grad, "tensor", axis=1, tiled=True)
    piece = (
        (
            all_out_grad.astype(f32).reshape(pairs, span, full_width)
            + all_pooled_grad[:, None, :] / span
        )
        .reshape(rows, full_width)
        .astype(bf16)
    )
    out_product = mm(piece, attended, TN).astype(bf16)
    attended_grad = mm(tie(piece, out_product), w_out, NT).astype(bf16)
    grads = [None] * pairs
    sent = None
    for index in reversed(range(pairs)):
        asked = queries[index] if sent is None else tie(queries[index], sent)
        grads[index] = attention(
            backward_kernel,
            5,
            cuts[index],
            asked,
            keys[index],
            keys[index + 1],
            values[index],
            values[index + 1],
            attended_grad[index * span : (index + 1) * span],
        )
        if index == pairs - 1:
            sent = jnp.concatenate([grads[index][2], grads[index][4]], 1)
            passed = from_behind(sent, "tm", 1)
    out_halves = halve_tm(out_product, position)
    small = lax.psum(
        jnp.concatenate([reward_part, term_part[:, None], gain_part[:, None]], 1).astype(bf16),
        "tm",
    ).astype(f32)
    grad_reward, grad_term, grad_gain = (
        small[:, :bins_count],
        small[:, bins_count],
        small[:, bins_count + 1],
    )
    query_grad = jnp.concatenate([grad[0] for grad in grads], 0)
    query_halves = halve_tm(mm(gathered, query_grad, TN).astype(bf16), position)

    def joined(first, second, behind):
        late = [behind] + [grad[second] for grad in grads[:-1]]
        return jnp.concatenate(
            [
                (grad[first].astype(f32) + other.astype(f32)).astype(bf16)
                for grad, other in zip(grads, late)
            ],
            0,
        )

    value_grad = joined(3, 4, passed[:, width:])
    value_halves = halve_tm(mm(gathered, value_grad, TN).astype(bf16), position)
    key_grad = joined(1, 2, passed[:, :width])
    key_halves = halve_tm(mm(gathered, key_grad, TN).astype(bf16), position)
    gives = (query_halves[1], value_halves[1], key_halves[1])
    grad_out = scatter_tm(out_halves, position, after=gives).T
    grad_query = scatter_tm(query_halves, position, twist, after=gives)
    grad_value = scatter_tm(value_halves, position, twist)
    grad_key = scatter_tm(key_halves, position, twist)
    return (
        mixed,
        pair_losses,
        grad_query,
        grad_key,
        grad_value,
        grad_out,
        grad_reward,
        grad_term,
        grad_gain,
    )


def solution(mesh):
    return jax.shard_map(
        local,
        mesh=mesh,
        in_specs=(
            P("tm", "tensor"),
            P(None, "tensor"),
            P(None, "tensor"),
            P(None, "tensor"),
            P("tensor", None),
            P("tensor"),
            P("tensor", None),
            P("tensor"),
            P("tm", "tensor"),
            P("tm"),
            P("tm"),
        ),
        out_specs=(
            P("tm", "tensor"),
            P(None, "tm"),
            P("tm", "tensor"),
            P("tm", "tensor"),
            P("tm", "tensor"),
            P("tensor", "tm"),
            P("tensor", None),
            P("tensor"),
            P("tensor"),
        ),
        check_vma=False,
    )
```
